32 devices in a mesh: segment: 2 (over x), dp: 4 (over z), mp: 4 (over y, core).
Axes of the slice: x: 2, y: 2, z: 4, core: 2. Of those that a mesh axis runs over, the one named last changes fastest.
Arguments:
- images: bfloat16 [8, 128, 3840], P(('segment', 'dp')), may hold values from -6 to 6
- ln_gain: float32 [1280], replicated, may hold values from 0.1 to 1.9
- projector: bfloat16 [3840, 8192], P(None, 'mp'), may hold values from -0.09375 to 0.09375
- tile_counts: int32 [8], P(('segment', 'dp')), may hold values from 1 to 4
- assign: int32 [8], P(('segment', 'dp')), may hold values from 0 to 7, as said below
- text: bfloat16 [8, 64, 8192], P('dp', None, 'mp'), may hold values from -6 to 6
- text_start: int32 [8], P('dp'), may hold values from 0 to 32
- w_query: bfloat16 [2, 8192, 4096], P('segment', 'mp'), may hold values from -0.0625 to 0.0625
- w_key: bfloat16 [2, 8192, 512], P('segment', 'mp'), may hold values from -0.0625 to 0.0625
- w_value: bfloat16 [2, 8192, 512], P('segment', 'mp'), may hold values from -0.0625 to 0.0625
- w_out: bfloat16 [2, 4096, 8192], P('segment', None, 'mp'), may hold values from -0.09375 to 0.09375
- gates: float32 [2], P('segment'), may hold values from -1.5 to 1.5
- grad_out: bfloat16 [8, 64, 8192], P('dp', None, 'mp'), may hold values from -6 to 6
Outputs:
- phase_grads: bfloat16 [2, 8, 64, 8192], P('segment', 'dp', None, 'mp')
- feature_grads: bfloat16 [8, 128, 3840], P(('segment', 'dp'))
The draws below stay inside these ranges and needn't reach their ends.
Inputs may be any that keep to these rules, and one draw needn't show every extreme that they name: assign is a permutation of the 8 sequences; sequence j belongs to index j // 2 of dp, image e is encoded on index e // 4 of segment and index e % 4 of dp, and the images of one index of segment belong to sequences of 4 different indices of dp.
All inputs are finite; a program needn't handle non-finite values.
Results may differ from the reference program's by a relative error of at most 0.035.
Values may be sent and summed in bfloat16 or wider, within the bound.
A program may use at most 192 MiB of HBM per device.

```python
import jax
import jax.numpy as jnp
from jax import lax

V = 1280
D = 8192
HQ = 32
KVH = 4
HD = 128
PATCH = 32
TXT = 64
R = 128
PROJ_IN = 3840
NIMG = 8
NSEQ = 8
N_SEGMENT = 2
N_DP = 4
N_MP = 4


def place_target(row, source, wanted):
    holder = jnp.argmax(row == wanted).astype(jnp.int32)
    moved = row[source]
    row = row.at[holder].set(moved)
    return row.at[source].set(wanted)


def draw_assign(key, part):
    group_key = jax.random.fold_in(key, 11)
    slot_key = jax.random.fold_in(key, 23)
    near_key = jax.random.fold_in(key, 37)
    far_key = jax.random.fold_in(key, 41)
    targets = jax.vmap(lambda subkey: jax.random.permutation(subkey, N_DP))(jax.random.split(group_key, N_SEGMENT)).astype(jnp.int32)
    near_source = jax.random.randint(near_key, (), 0, N_DP).astype(jnp.int32)
    far_source = jax.random.randint(far_key, (), 0, N_DP).astype(jnp.int32)
    first_row = place_target(targets[0], near_source, (near_source + 1) % N_DP)
    targets = targets.at[0].set(first_row)
    last_row = place_target(targets[N_SEGMENT - 1], far_source, (far_source + N_DP // 2) % N_DP)
    targets = targets.at[N_SEGMENT - 1].set(last_row)
    places = jax.vmap(lambda subkey: jax.random.permutation(subkey, N_SEGMENT))(jax.random.split(slot_key, N_DP)).astype(jnp.int32)
    segment_ids = jnp.broadcast_to(jnp.arange(N_SEGMENT, dtype=jnp.int32)[:, None], (N_SEGMENT, N_DP))
    slot_of = places[targets, segment_ids]
    return (targets * N_SEGMENT + slot_of).reshape(-1).astype(jnp.int32)


def place_ends(array, rng, least, largest):
    longest = array.shape.index(max(array.shape))
    spots = []
    for shift in (0, 1):
        where = [jax.random.randint(jax.random.fold_in(rng, axis), (), 0, length) for axis, length in enumerate(array.shape)]
        where[longest] = (where[longest] + shift) % array.shape[longest]
        spots.append(tuple(where))
    return array.at[spots[0]].set(least).at[spots[1]].set(largest)


def steps_of(rng, shape, cuts, low, largest):
    factor_of, own = 1.0, jax.random.fold_in(rng, 6)
    for dim, blocks in cuts:
        steps = jnp.exp(jax.random.uniform(jax.random.fold_in(own, dim), (blocks,), jnp.float32, low / len(cuts), largest / len(cuts)))
        factor_of = factor_of * jnp.repeat(steps, shape[dim] // blocks).reshape([-1 if axis == dim else 1 for axis in range(len(shape))])
    return factor_of


def scatter_about(rng, extent, spread, most, pieces=(), kind=jnp.bfloat16):
    factor_of = steps_of(rng, extent, pieces, -0.22, 0.18) if pieces else 1.0
    array = jax.random.normal(rng, extent, jnp.float32) * spread * factor_of
    return jnp.minimum(jnp.maximum(array, -most), most).astype(kind)


def setup_inputs(seed: int = 0) -> dict:
    key_of = jax.random.split(jax.random.key(seed), 14)
    return {
        "images": scatter_about(key_of[0], (NIMG, R, PROJ_IN), 1.0, 6.0, ((0, 8),)),
        "ln_gain": jnp.clip(1.0 + 0.18 * jax.random.normal(key_of[1], (V,), jnp.float32), 0.1, 1.9),
        "projector": scatter_about(key_of[2], (PROJ_IN, D), PROJ_IN ** -0.5, 0.09375, ((1, 4),)),
        "tile_counts": place_ends(jax.random.randint(key_of[3], (NIMG,), 1, 5), jax.random.fold_in(key_of[3], 1), 1, 4).astype(jnp.int32),
        "assign": draw_assign(jax.random.fold_in(key_of[13], 71), 0),
        "text": scatter_about(key_of[5], (NSEQ, TXT, D), 1.0, 6.0, ((0, 4), (2, 4))),
        "text_start": place_ends(jax.random.randint(key_of[6], (NSEQ,), 0, TXT // 2 + 1), jax.random.fold_in(key_of[6], 1), 0, (TXT // 2 + 1) - 1).astype(jnp.int32),
        "w_query": scatter_about(key_of[7], (N_SEGMENT, D, HQ * HD), D ** -0.5, 0.0625, ((0, 2), (1, 4))),
        "w_key": scatter_about(key_of[8], (N_SEGMENT, D, KVH * HD), D ** -0.5, 0.0625, ((0, 2), (1, 4))),
        "w_value": scatter_about(key_of[9], (N_SEGMENT, D, KVH * HD), D ** -0.5, 0.0625, ((0, 2), (1, 4))),
        "w_out": scatter_about(key_of[10], (N_SEGMENT, HQ * HD, D), (HQ * HD) ** -0.5, 0.09375, ((0, 2), (2, 4))),
        "gates": jnp.clip(jax.random.uniform(key_of[11], (N_SEGMENT,), jnp.float32, -1.5, 1.5) * steps_of(key_of[11], (N_SEGMENT,), ((0, 2),), -0.4, 0.0), -1.5, 1.5),
        "grad_out": scatter_about(key_of[12], (NSEQ, TXT, D), 1.0, 6.0, ((0, 4), (2, 4))),
    }


def to_half_and_back(value):
    return lax.optimization_barrier(value.astype(jnp.bfloat16)).astype(jnp.float32)

def block_sum(left, right):
    block_width = D // N_MP
    left_blocks = left.reshape(NSEQ, TXT, N_MP, block_width).astype(jnp.float32)
    right_blocks = right.reshape(N_MP, block_width, -1).astype(jnp.float32)
    partial_value = jnp.einsum('stmc,mcf->mstf', left_blocks, right_blocks)
    return to_half_and_back(partial_value).sum(0).astype(jnp.bfloat16)

def block_sum_back(left, right):
    block_width = D // N_MP
    left_blocks = left.reshape(NSEQ, TXT, N_MP, block_width).astype(jnp.float32)
    right_blocks = right.reshape(-1, N_MP, block_width).astype(jnp.float32)
    partial_value = jnp.einsum('stmc,fmc->mstf', left_blocks, right_blocks)
    return to_half_and_back(partial_value).sum(0).astype(jnp.bfloat16)

def masked_softmax(scores, key_mask):
    scores = jnp.where(key_mask, scores, -1e+30)
    row_top = lax.optimization_barrier(jnp.max(scores, axis=-1, keepdims=True))
    raised = jnp.exp(scores - row_top)
    return raised / lax.optimization_barrier(jnp.sum(raised, axis=-1, keepdims=True))

def reference(images, ln_gain, projector, tile_counts, assign, text, text_start, w_query, w_key, w_value, w_out, gates, grad_out):
    last_cols = images[:, :, :V].astype(jnp.float32)
    center = last_cols - lax.optimization_barrier(jnp.mean(last_cols, axis=-1, keepdims=True))
    variance = lax.optimization_barrier(jnp.mean(center * center, axis=-1, keepdims=True))
    inv_std = lax.rsqrt(variance + 1e-05)
    normed = center * inv_std
    tile_norm = (normed * ln_gain).astype(jnp.bfloat16)
    tile_in = jnp.concatenate([tile_norm, images[:, :, V:]], axis=2)
    features = jnp.einsum('erv,vc->erc', tile_in.astype(jnp.float32), projector.astype(jnp.float32)).astype(jnp.bfloat16)
    image_of = jnp.zeros((NSEQ,), jnp.int32).at[assign].set(jnp.arange(NIMG, dtype=jnp.int32))
    seq_features = features[image_of]
    seq_tiles = tile_counts[image_of]
    key_mask = (jnp.arange(R, dtype=jnp.int32)[None, :] < seq_tiles[:, None] * PATCH)[:, None, None, :]
    text_live = (jnp.arange(TXT, dtype=jnp.int32)[None, :] >= text_start[:, None]).astype(jnp.float32)[:, :, None]
    score_scale = HD ** (-0.5)
    group_size = HQ // KVH
    feat_wide = seq_features.astype(jnp.float32)
    hidden = text
    saved = []
    for layer in range(N_SEGMENT):
        query = block_sum(hidden, w_query[layer])
        keys = jnp.einsum('src,cf->srf', feat_wide, w_key[layer].astype(jnp.float32)).astype(jnp.bfloat16)
        values = jnp.einsum('src,cf->srf', feat_wide, w_value[layer].astype(jnp.float32)).astype(jnp.bfloat16)
        key_heads = jnp.repeat(keys.reshape(NSEQ, R, KVH, HD), group_size, axis=2).astype(jnp.float32)
        value_heads = jnp.repeat(values.reshape(NSEQ, R, KVH, HD), group_size, axis=2).astype(jnp.float32)
        query_heads = query.reshape(NSEQ, TXT, HQ, HD).astype(jnp.float32)
        scores = jnp.einsum('sthd,srhd->shtr', query_heads, key_heads) * score_scale
        probs = masked_softmax(scores, key_mask)
        weights = probs.astype(jnp.bfloat16)
        mixed = jnp.einsum('shtr,srhd->sthd', weights.astype(jnp.float32), value_heads).astype(jnp.bfloat16).reshape(NSEQ, TXT, HQ * HD)
        projected = jnp.einsum('stf,fc->stc', mixed.astype(jnp.float32), w_out[layer].astype(jnp.float32))
        saved.append((query_heads, key_heads, value_heads, probs, weights))
        hidden = (hidden.astype(jnp.float32) + jnp.tanh(gates[layer]) * text_live * projected).astype(jnp.bfloat16)
    cotangent = grad_out
    grads_list = [None] * N_SEGMENT
    feature_total = jnp.zeros((NSEQ, R, D), jnp.float32)
    for layer in range(N_SEGMENT - 1, -1, -1):
        query_heads, key_heads, value_heads, probs, weights = saved[layer]
        out_cot = (jnp.tanh(gates[layer]) * text_live * cotangent.astype(jnp.float32)).astype(jnp.bfloat16)
        mixed_cot = block_sum_back(out_cot, w_out[layer])
        mixed_heads = mixed_cot.reshape(NSEQ, TXT, HQ, HD).astype(jnp.float32)
        prob_cot = jnp.einsum('sthd,srhd->shtr', mixed_heads, value_heads)
        score_cot = probs * (prob_cot - lax.optimization_barrier(jnp.sum(prob_cot * probs, axis=-1, keepdims=True))) * score_scale
        score_cot = to_half_and_back(score_cot)
        query_cot = jnp.einsum('shtr,srhd->sthd', score_cot, key_heads).astype(jnp.bfloat16).reshape(NSEQ, TXT, HQ * HD)
        key_cot = jnp.einsum('shtr,sthd->srhd', score_cot, query_heads).reshape(NSEQ, R, KVH, group_size, HD).sum(3)
        value_cot = jnp.einsum('shtr,sthd->srhd', weights.astype(jnp.float32), mixed_heads).reshape(NSEQ, R, KVH, group_size, HD).sum(3)
        key_cot = to_half_and_back(key_cot.reshape(NSEQ, R, KVH * HD))
        value_cot = to_half_and_back(value_cot.reshape(NSEQ, R, KVH * HD))
        cotangent = (cotangent.astype(jnp.float32) + jnp.einsum('stf,cf->stc', query_cot.astype(jnp.float32), w_query[layer].astype(jnp.float32))).astype(jnp.bfloat16)
        grads_list[layer] = cotangent
        feature_cot = jnp.einsum('srf,cf->src', key_cot, w_key[layer].astype(jnp.float32)) + jnp.einsum('srf,cf->src', value_cot, w_value[layer].astype(jnp.float32))
        feature_total = feature_total + to_half_and_back(feature_cot)
    feature_cot = feature_total.astype(jnp.bfloat16)[assign]
    norm_cot = jnp.einsum('erc,vc->erv', feature_cot.astype(jnp.float32), projector.astype(jnp.float32))
    scaled = norm_cot[:, :, :V] * ln_gain
    last_grad = inv_std * (scaled - lax.optimization_barrier(jnp.mean(scaled, axis=-1, keepdims=True)) - normed * lax.optimization_barrier(jnp.mean(scaled * normed, axis=-1, keepdims=True)))
    result = jnp.concatenate([last_grad, norm_cot[:, :, V:]], axis=2)
    return (jnp.stack(grads_list), result.astype(jnp.bfloat16))
```

```python
import jax
import jax.numpy as jnp
from jax import lax
from jax.sharding import PartitionSpec as P

HD = 128
PATCH = 32
BF = jnp.bfloat16
F32 = jnp.float32


def swap(value, axis, bit):
    count = lax.axis_size(axis)
    return lax.ppermute(value, axis, [(i, i ^ bit) for i in range(count)])


def pick(array, index, axis=0):
    return lax.dynamic_index_in_dim(array, index, axis, keepdims=False)


def scatter_sum(parts, axis="mp"):
    index = lax.axis_index(axis)
    low, high = index % 2, index // 2
    pairs = parts.reshape((2, 2) + parts.shape[1:])
    kept = pick(pairs, low, 1) + swap(pick(pairs, 1 - low, 1).astype(BF), axis, 1).astype(F32)
    return pick(kept, high, 0) + swap(pick(kept, 1 - high, 0).astype(BF), axis, 2).astype(F32)


def scatter_columns(part):
    rows, width = part.shape
    count = lax.axis_size("mp")
    index = lax.axis_index("mp")
    low, high = index % 2, index // 2
    n = width // count

    def block(array, k):
        return lax.dynamic_slice_in_dim(array, k * n, n, 1)

    sent = jnp.concatenate([block(part, 1 - low), block(part, 3 - low)], axis=1).astype(BF)
    got = swap(sent, "mp", 1).astype(F32)
    mine = block(part, 2 * high + low) + block(got, high)
    other = block(part, 2 * (1 - high) + low) + block(got, 1 - high)
    return mine + swap(other.astype(BF), "mp", 2).astype(F32)


def softmax_rows(query, keys, key_mask):
    scores = jnp.einsum("bqd,brd->bqr", query, keys, preferred_element_type=F32) * HD ** (-0.5)
    scores = jnp.where(key_mask[:, None, :], scores, -1e30)
    raised = jnp.exp(scores - jnp.max(scores, axis=-1, keepdims=True))
    return raised / jnp.sum(raised, axis=-1, keepdims=True)


def attend_back(query, mixed_cot, keys, values, key_mask):
    probs = softmax_rows(query, keys, key_mask)
    prob_cot = jnp.einsum("bqd,brd->bqr", mixed_cot, values, preferred_element_type=F32)
    score_cot = (
        probs * (prob_cot - jnp.sum(prob_cot * probs, axis=-1, keepdims=True)) * HD ** (-0.5)
    ).astype(BF)
    query_cot = jnp.einsum("bqr,brd->bqd", score_cot, keys, preferred_element_type=F32).astype(BF)
    key_cot = jnp.einsum("bqr,bqd->brd", score_cot, query, preferred_element_type=F32)
    value_cot = jnp.einsum("bqr,bqd->brd", probs.astype(BF), mixed_cot, preferred_element_type=F32)
    return query_cot, jnp.concatenate([key_cot, value_cot], axis=-1).astype(BF)


def times_transposed(value, weight):
    return lax.dot_general(value, weight, (((1,), (1,)), ((), ())), preferred_element_type=F32)


def local(
    images,
    ln_gain,
    projector,
    tile_counts,
    assign,
    text,
    text_start,
    w_query,
    w_key,
    w_value,
    w_out,
    gates,
    grad_out,
):
    segments = lax.axis_size("segment")
    groups = lax.axis_size("dp")
    members = lax.axis_size("mp")
    segment_id = lax.axis_index("segment")
    group_id = lax.axis_index("dp")
    member_id = lax.axis_index("mp")
    micro, length, feat_width = text.shape
    rows_img, proj_in = images.shape[1:]
    last_width = ln_gain.shape[0]
    query_width = w_query.shape[2]
    share = rows_img // members
    tokens = micro * length
    first = segment_id == 0
    gate_value = jnp.tanh(gates[0])
    query_weight, out_weight = w_query[0], w_out[0]
    key_weight, value_weight = w_key[0], w_value[0]
    kv_width = key_weight.shape[1]

    own_rows = lax.dynamic_slice_in_dim(images[0], member_id * share, share, 0)
    last_cols = own_rows[:, :last_width].astype(F32)
    center = last_cols - jnp.mean(last_cols, axis=-1, keepdims=True)
    inv_std = lax.rsqrt(jnp.mean(center * center, axis=-1, keepdims=True) + 1e-05)
    normed = center * inv_std
    tile_rows = jnp.concatenate([(normed * ln_gain).astype(BF), own_rows[:, last_width:]], axis=1)

    table = lax.all_gather(
        jnp.concatenate([assign, tile_counts])[None], ("segment", "dp"), axis=0, tiled=True
    ).reshape(segments, groups, 2)
    assigned, tiles = table[:, :, 0], table[:, :, 1]
    here = assigned // micro == group_id
    source = jnp.argmax(here, axis=1).astype(jnp.int32)
    slot_of = jnp.sum(jnp.where(here, assigned % micro, 0), axis=1)
    tiles_of = jnp.sum(jnp.where(here, tiles, 0), axis=1)
    seq_ids = jnp.arange(micro, dtype=jnp.int32)
    chosen = slot_of[None, :] == seq_ids[:, None]
    image_seg = jnp.argmax(chosen, axis=1).astype(jnp.int32)
    counts = jnp.sum(jnp.where(chosen, tiles_of[None, :], 0), axis=1)
    key_mask = jnp.arange(rows_img, dtype=jnp.int32)[None, :] < counts[:, None] * PATCH
    text_live = (
        jnp.arange(length, dtype=jnp.int32)[None, :] >= text_start[:, None]
    ).astype(F32)
    scale = (gate_value * text_live).reshape(tokens, 1)

    column = lax.all_gather(tile_rows, "dp", axis=0, tiled=False)
    mine = pick(column, pick(source, segment_id))
    tile_in = lax.all_gather(mine, ("segment", "mp"), axis=0, tiled=True)

    text_rows = text.reshape(tokens, feat_width)
    grad_rows = grad_out.reshape(tokens, feat_width)
    out_cot = (scale * grad_rows.astype(F32)).astype(BF)
    early = lax.cond(
        first,
        lambda: jnp.dot(text_rows, query_weight, preferred_element_type=F32),
        lambda: times_transposed(out_cot, out_weight),
    )
    early_sum = scatter_columns(early).astype(BF)

    def heads(array):
        return array.reshape(micro, -1, HD)

    def flat(array):
        return array.reshape(tokens, -1)

    features = jnp.dot(tile_in, projector, preferred_element_type=F32).astype(BF)
    key_part = jnp.dot(features, key_weight, preferred_element_type=F32)
    value_part = jnp.dot(features, value_weight, preferred_element_type=F32)
    per = kv_width // members
    parts = jnp.stack([key_part, value_part]).reshape(2, -1, members, per).transpose(2, 0, 1, 3)
    kv_image = scatter_sum(parts).astype(BF).reshape(2, segments, rows_img, per)
    kv = jnp.stack([pick(kv_image, image_seg[i], 1) for i in range(micro)], axis=1)
    keys, values = kv[0], kv[1]

    probs = softmax_rows(heads(early_sum), keys, key_mask)
    mixed = jnp.einsum("bqr,brd->bqd", probs.astype(BF), values, preferred_element_type=F32)
    mixed_all = lax.all_gather(flat(mixed.astype(BF)), "mp", axis=1, tiled=True)
    projected = jnp.dot(mixed_all, out_weight, preferred_element_type=F32)
    hidden = (text_rows.astype(F32) + scale * projected).astype(BF)
    hidden = swap(hidden, "segment", 1)

    query_late = scatter_columns(
        jnp.dot(hidden, query_weight, preferred_element_type=F32)
    ).astype(BF)
    query_cot, kv_cot_late = attend_back(
        heads(query_late), heads(early_sum), keys, values, key_mask
    )
    query_back = times_transposed(
        lax.all_gather(flat(query_cot), "mp", axis=1, tiled=True), query_weight
    )
    cot_late = (grad_rows.astype(F32) + query_back).astype(BF)
    cot_in = swap(cot_late, "segment", 1)

    out_cot = (scale * cot_in.astype(F32)).astype(BF)
    mixed_cot = scatter_columns(times_transposed(out_cot, out_weight)).astype(BF)
    query_cot, kv_cot_early = attend_back(
        heads(early_sum), heads(mixed_cot), keys, values, key_mask
    )
    kv_cot = jnp.where(first, kv_cot_early, kv_cot_late)
    kv_cot = jnp.stack([pick(kv_cot, slot_of[i]) for i in range(segments)])
    kv_all = lax.all_gather(kv_cot.reshape(segments * rows_img, 2 * per), "mp", axis=0)
    query_back = times_transposed(
        lax.all_gather(flat(query_cot), "mp", axis=1, tiled=True), query_weight
    )
    cot_early = (cot_in.astype(F32) + query_back).astype(BF)
    grads = jnp.where(first, cot_early, cot_late)

    key_all = kv_all[:, :, :per].transpose(1, 0, 2).reshape(-1, kv_width)
    value_all = kv_all[:, :, per:].transpose(1, 0, 2).reshape(-1, kv_width)
    feature_cot = (
        times_transposed(key_all, key_weight) + times_transposed(value_all, value_weight)
    ).astype(BF)
    norm_part = times_transposed(feature_cot, projector)
    parts = norm_part.reshape(segments, members, share, proj_in).transpose(1, 0, 2, 3)
    summed = scatter_sum(parts)
    returned = pick(summed, segment_id) + swap(
        pick(summed, 1 - segment_id).astype(BF), "segment", 1
    ).astype(F32)
    column = lax.all_gather(returned.astype(BF), "dp", axis=0, tiled=False)
    norm_cot = pick(column, assign[0] // micro).astype(F32)
    scaled = norm_cot[:, :last_width] * ln_gain
    last_grad = inv_std * (
        scaled
        - jnp.mean(scaled, axis=-1, keepdims=True)
        - normed * jnp.mean(scaled * normed, axis=-1, keepdims=True)
    )
    result = jnp.concatenate([last_grad, norm_cot[:, last_width:]], axis=1).astype(BF)
    result = lax.all_gather(result, "mp", axis=0, tiled=True)
    return (grads.reshape(1, micro, length, feat_width), result[None])


def solution(mesh):
    return jax.shard_map(
        local,
        mesh=mesh,
        in_specs=(
            P(("segment", "dp"), None, None),
            P(),
            P(None, "mp"),
            P(("segment", "dp")),
            P(("segment", "dp")),
            P("dp", None, "mp"),
            P("dp"),
            P("segment", "mp", None),
            P("segment", "mp", None),
            P("segment", "mp", None),
            P("segment", None, "mp"),
            P("segment"),
            P("dp", None, "mp"),
        ),
        out_specs=(P("segment", "dp", None, "mp"), P(("segment", "dp"), None, None)),
        check_vma=False,
    )
```

```python
import jax
import jax.numpy as jnp
from jax import lax
from jax.sharding import PartitionSpec as P

HD = 128
PATCH = 32
CHUNKS = 2
LANES = 512
BF = jnp.bfloat16
F32 = jnp.float32


def swap(value, axis, bit):
    count = lax.axis_size(axis)
    return lax.ppermute(value, axis, [(i, i ^ bit) for i in range(count)])


def pick(array, index, axis=0):
    return lax.dynamic_index_in_dim(array, index, axis, keepdims=False)


def scatter_sum(parts, axis="mp"):
    index = lax.axis_index(axis)
    low, high = index % 2, index // 2
    pairs = parts.reshape((2, 2) + parts.shape[1:])
    kept = pick(pairs, low, 1) + swap(pick(pairs, 1 - low, 1).astype(BF), axis, 1).astype(F32)
    return pick(kept, high, 0) + swap(pick(kept, 1 - high, 0).astype(BF), axis, 2).astype(F32)


def scatter_columns(part):
    rows, width = part.shape
    count = lax.axis_size("mp")
    index = lax.axis_index("mp")
    low, high = index % 2, index // 2
    n = width // count

    def block(array, k):
        return lax.dynamic_slice_in_dim(array, k * n, n, 1)

    sent = jnp.concatenate([block(part, 1 - low), block(part, 3 - low)], axis=1).astype(BF)
    got = swap(sent, "mp", 1).astype(F32)
    mine = block(part, 2 * high + low) + block(got, high)
    other = block(part, 2 * (1 - high) + low) + block(got, 1 - high)
    return mine + swap(other.astype(BF), "mp", 2).astype(F32)


def gather_pairs(block):
    index = lax.axis_index("mp")
    low = index % 2
    across = swap(block, "mp", 2)
    near = swap(block, "mp", 1)
    far = swap(across, "mp", 1)

    def side_by_side(own, other):
        return jnp.concatenate(
            [jnp.where(low == 0, own, other), jnp.where(low == 0, other, own)], axis=1
        )

    return side_by_side(block, near), side_by_side(across, far)


def gathered_product(block, weight, transposed):
    near, far = gather_pairs(block)
    high = lax.axis_index("mp") // 2
    depth = near.shape[1]
    axis, width = (1, weight.shape[0]) if transposed else (0, weight.shape[1])
    size = width // CHUNKS
    first = lax.dynamic_slice_in_dim(weight, high * depth, depth, axis)
    second = lax.dynamic_slice_in_dim(weight, (1 - high) * depth, depth, axis)
    multiply = times_transposed if transposed else dot
    started = multiply(near, first)
    result = []
    for c in range(CHUNKS):
        part = lax.slice_in_dim(second, c * size, (c + 1) * size, axis=1 - axis)
        result.append(started[:, c * size : (c + 1) * size] + multiply(far, part))
    return result


def chunked_product(chunks, weight, transposed):
    size = weight.shape[1 if transposed else 0] // CHUNKS
    total = None
    for c, chunk in enumerate(chunks):
        part = lax.slice_in_dim(weight, c * size, (c + 1) * size, axis=1 if transposed else 0)
        product = (times_transposed if transposed else dot)(chunk, part)
        total = product if total is None else total + product
    return total


def split(array):
    return jnp.split(array, CHUNKS, axis=1)


def dot(value, weight):
    return jnp.dot(value, weight, preferred_element_type=F32)


def softmax_rows(query, keys, key_mask):
    scores = jnp.einsum("bqd,brd->bqr", query, keys, preferred_element_type=F32) * HD ** (-0.5)
    scores = jnp.where(key_mask[:, None, :], scores, -1e30)
    raised = jnp.exp(scores - jnp.max(scores, axis=-1, keepdims=True))
    return raised / jnp.sum(raised, axis=-1, keepdims=True)


def attend_back(query, mixed_cot, keys, values, key_mask):
    probs = softmax_rows(query, keys, key_mask)
    prob_cot = jnp.einsum("bqd,brd->bqr", mixed_cot, values, preferred_element_type=F32)
    score_cot = (
        probs * (prob_cot - jnp.sum(prob_cot * probs, axis=-1, keepdims=True)) * HD ** (-0.5)
    ).astype(BF)
    query_cot = jnp.einsum("bqr,brd->bqd", score_cot, keys, preferred_element_type=F32).astype(BF)
    key_cot = jnp.einsum("bqr,bqd->brd", score_cot, query, preferred_element_type=F32)
    value_cot = jnp.einsum("bqr,bqd->brd", probs.astype(BF), mixed_cot, preferred_element_type=F32)
    return query_cot, jnp.concatenate([key_cot, value_cot], axis=-1).astype(BF)


def times_transposed(value, weight):
    return lax.dot_general(value, weight, (((1,), (1,)), ((), ())), preferred_element_type=F32)


def local(
    images,
    ln_gain,
    projector,
    tile_counts,
    assign,
    text,
    text_start,
    w_query,
    w_key,
    w_value,
    w_out,
    gates,
    grad_out,
):
    segments = lax.axis_size("segment")
    groups = lax.axis_size("dp")
    members = lax.axis_size("mp")
    segment_id = lax.axis_index("segment")
    group_id = lax.axis_index("dp")
    member_id = lax.axis_index("mp")
    micro, length, feat_width = text.shape
    rows_img, proj_in = images.shape[1:]
    last_width = ln_gain.shape[0]
    query_width = w_query.shape[2]
    share = rows_img // members
    tokens = micro * length
    first = segment_id == 0
    gate_value = jnp.tanh(gates[0])
    query_weight, out_weight = w_query[0], w_out[0]
    key_weight, value_weight = w_key[0], w_value[0]
    kv_width = key_weight.shape[1]

    own_rows = lax.dynamic_slice_in_dim(images[0], member_id * share, share, 0)
    last_cols = own_rows[:, :last_width].astype(F32)
    center = last_cols - jnp.mean(last_cols, axis=-1, keepdims=True)
    inv_std = lax.rsqrt(jnp.mean(center * center, axis=-1, keepdims=True) + 1e-05)
    normed = center * inv_std
    tile_rows = jnp.concatenate([(normed * ln_gain).astype(BF), own_rows[:, last_width:]], axis=1)

    proj_pad = (-proj_in) % LANES or LANES
    facts = jnp.concatenate([assign, tile_counts]).astype(BF)
    facts = jnp.broadcast_to(facts[None], (share, 2))
    sent = jnp.concatenate(
        [tile_rows, jnp.pad(facts, ((0, 0), (0, proj_pad - 2)))], axis=1
    )
    column = lax.all_gather(sent, "dp", axis=0, tiled=False)
    there = column[:, 0, proj_in].astype(jnp.int32)
    source = jnp.argmax(there // micro == group_id).astype(jnp.int32)
    arrived = lax.all_gather(pick(column, source), ("segment", "mp"), axis=0, tiled=True)
    arrived_facts = arrived.reshape(segments, rows_img, -1)[:, 0, proj_in:].astype(jnp.int32)
    slot_of = arrived_facts[:, 0] % micro
    tiles_of = arrived_facts[:, 1]
    tile_in = arrived[:, :proj_in]

    seq_ids = jnp.arange(micro, dtype=jnp.int32)
    chosen = slot_of[None, :] == seq_ids[:, None]
    image_seg = jnp.argmax(chosen, axis=1).astype(jnp.int32)
    counts = jnp.sum(jnp.where(chosen, tiles_of[None, :], 0), axis=1)
    key_mask = jnp.arange(rows_img, dtype=jnp.int32)[None, :] < counts[:, None] * PATCH
    text_live = (
        jnp.arange(length, dtype=jnp.int32)[None, :] >= text_start[:, None]
    ).astype(F32)
    scale = (gate_value * text_live).reshape(tokens, 1)

    text_rows = text.reshape(tokens, feat_width)
    grad_rows = grad_out.reshape(tokens, feat_width)
    out_cot = (scale * grad_rows.astype(F32)).astype(BF)
    early = lax.cond(
        first,
        lambda: jnp.dot(text_rows, query_weight, preferred_element_type=F32),
        lambda: times_transposed(out_cot, out_weight),
    )
    early_sum = scatter_columns(early).astype(BF)

    def heads(array):
        return array.reshape(micro, -1, HD)

    def flat(array):
        return array.reshape(tokens, -1)

    features = jnp.dot(tile_in, projector, preferred_element_type=F32).astype(BF)
    key_part = jnp.dot(features, key_weight, preferred_element_type=F32)
    value_part = jnp.dot(features, value_weight, preferred_element_type=F32)
    per = kv_width // members
    parts = jnp.stack([key_part, value_part]).reshape(2, -1, members, per).transpose(2, 0, 1, 3)
    kv_image = scatter_sum(parts).astype(BF).reshape(2, segments, rows_img, per)
    kv = jnp.stack([pick(kv_image, image_seg[i], 1) for i in range(micro)], axis=1)
    keys, values = kv[0], kv[1]

    probs = softmax_rows(heads(early_sum), keys, key_mask)
    mixed = jnp.einsum("bqr,brd->bqd", probs.astype(BF), values, preferred_element_type=F32)
    projected = gathered_product(flat(mixed.astype(BF)), out_weight, False)
    hidden = [
        swap((t.astype(F32) + scale * p).astype(BF), "segment", 1)
        for t, p in zip(split(text_rows), projected)
    ]

    query_late = scatter_columns(chunked_product(hidden, query_weight, False)).astype(BF)
    query_cot, kv_cot_late = attend_back(
        heads(query_late), heads(early_sum), keys, values, key_mask
    )
    query_back = gathered_product(flat(query_cot), query_weight, True)
    cot_late = [(g.astype(F32) + q).astype(BF) for g, q in zip(split(grad_rows), query_back)]
    cot_in = [swap(c, "segment", 1) for c in cot_late]

    out_cot = [(scale * c.astype(F32)).astype(BF) for c in cot_in]
    mixed_cot = scatter_columns(chunked_product(out_cot, out_weight, True)).astype(BF)
    query_cot, kv_cot_early = attend_back(
        heads(early_sum), heads(mixed_cot), keys, values, key_mask
    )
    kv_cot = jnp.where(first, kv_cot_early, kv_cot_late)
    kv_cot = jnp.stack([pick(kv_cot, slot_of[i]) for i in range(segments)])
    kv_all = lax.all_gather(kv_cot.reshape(segments * rows_img, 2 * per), "mp", axis=0)
    near, far = gather_pairs(flat(query_cot))
    high = member_id // 2
    gathered = jnp.concatenate(
        [jnp.where(high == 0, near, far), jnp.where(high == 0, far, near)], axis=1
    )
    query_back = times_transposed(gathered, query_weight)
    cot_early = (jnp.concatenate(cot_in, axis=1).astype(F32) + query_back).astype(BF)
    grads = jnp.where(first, cot_early, jnp.concatenate(cot_late, axis=1))

    key_all = kv_all[:, :, :per].transpose(1, 0, 2).reshape(-1, kv_width)
    value_all = kv_all[:, :, per:].transpose(1, 0, 2).reshape(-1, kv_width)
    feature_cot = (
        times_transposed(key_all, key_weight) + times_transposed(value_all, value_weight)
    ).astype(BF)
    norm_part = times_transposed(feature_cot, projector)
    parts = norm_part.reshape(segments, members, share, proj_in).transpose(1, 0, 2, 3)
    summed = scatter_sum(parts)
    returned = pick(summed, segment_id) + swap(
        pick(summed, 1 - segment_id).astype(BF), "segment", 1
    ).astype(F32)
    column = lax.all_gather(
        jnp.pad(returned.astype(BF), ((0, 0), (0, proj_pad))), "dp", axis=0, tiled=False
    )
    norm_cot = pick(column, assign[0] // micro)[:, :proj_in].astype(F32)
    scaled = norm_cot[:, :last_width] * ln_gain
    last_grad = inv_std * (
        scaled
        - jnp.mean(scaled, axis=-1, keepdims=True)
        - normed * jnp.mean(scaled * normed, axis=-1, keepdims=True)
    )
    result = jnp.concatenate([last_grad, norm_cot[:, last_width:]], axis=1).astype(BF)
    result = lax.all_gather(result, "mp", axis=0, tiled=True)
    return (grads.reshape(1, micro, length, feat_width), result[None])


def solution(mesh):
    return jax.shard_map(
        local,
        mesh=mesh,
        in_specs=(
            P(("segment", "dp"), None, None),
            P(),
            P(None, "mp"),
            P(("segment", "dp")),
            P(("segment", "dp")),
            P("dp", None, "mp"),
            P("dp"),
            P("segment", "mp", None),
            P("segment", "mp", None),
            P("segment", "mp", None),
            P("segment", None, "mp"),
            P("segment"),
            P("dp", None, "mp"),
        ),
        out_specs=(P("segment", "dp", None, "mp"), P(("segment", "dp"), None, None)),
        check_vma=False,
    )
```

```python
import functools

import jax
import jax.numpy as jnp
from jax import lax
from jax.experimental import pallas as pl
from jax.experimental.pallas import tpu as pltpu
from jax.sharding import PartitionSpec as P

HD = 128
PATCH = 32
CHUNKS = 2
LANES = 128
BACK_LANES = 512
BLOCK = 2**20
BF = jnp.bfloat16
F32 = jnp.float32


def swap(value, axis, bit):
    count = lax.axis_size(axis)
    return lax.ppermute(value, axis, [(i, i ^ bit) for i in range(count)])


def pick(array, index, axis=0):
    return lax.dynamic_index_in_dim(array, index, axis, keepdims=False)


def scatter_sum(parts, axis="mp"):
    index = lax.axis_index(axis)
    low, high = index % 2, index // 2
    pairs = parts.reshape((2, 2) + parts.shape[1:])
    kept = pick(pairs, low, 1) + swap(pick(pairs, 1 - low, 1).astype(BF), axis, 1).astype(F32)
    return pick(kept, high, 0) + swap(pick(kept, 1 - high, 0).astype(BF), axis, 2).astype(F32)


def scatter_columns(part):
    rows, width = part.shape
    count = lax.axis_size("mp")
    index = lax.axis_index("mp")
    low, high = index % 2, index // 2
    n = width // count

    def block(array, k):
        return lax.dynamic_slice_in_dim(array, k * n, n, 1)

    sent = jnp.concatenate([block(part, 1 - low), block(part, 3 - low)], axis=1).astype(BF)
    got = swap(sent, "mp", 1).astype(F32)
    mine = block(part, 2 * high + low) + block(got, high)
    other = block(part, 2 * (1 - high) + low) + block(got, 1 - high)
    return mine + swap(other.astype(BF), "mp", 2).astype(F32)


def gather_pairs(block):
    index = lax.axis_index("mp")
    low = index % 2
    across = swap(block, "mp", 2)
    near = swap(block, "mp", 1)
    far = swap(across, "mp", 1)

    def side_by_side(own, other):
        return jnp.concatenate(
            [jnp.where(low == 0, own, other), jnp.where(low == 0, other, own)], axis=1
        )

    return side_by_side(block, near), side_by_side(across, far)


def gathered_product(block, weight, transposed):
    near, far = gather_pairs(block)
    high = lax.axis_index("mp") // 2
    depth = near.shape[1]
    axis, width = (1, weight.shape[0]) if transposed else (0, weight.shape[1])
    size = width // CHUNKS
    first = lax.dynamic_slice_in_dim(weight, high * depth, depth, axis)
    multiply = times_transposed if transposed else dot
    started = multiply(near, first)
    result = []
    for c in range(CHUNKS):
        corner, shape = [c * size] * 2, [size] * 2
        corner[axis], shape[axis] = (1 - high) * depth, depth
        part = lax.dynamic_slice(weight, corner, shape)
        result.append(started[:, c * size : (c + 1) * size] + multiply(far, part))
    return result


def chunked_product(chunks, weight, transposed):
    size = weight.shape[1 if transposed else 0] // CHUNKS
    total = None
    for c, chunk in enumerate(chunks):
        part = lax.slice_in_dim(weight, c * size, (c + 1) * size, axis=1 if transposed else 0)
        product = (times_transposed if transposed else dot)(chunk, part)
        total = product if total is None else total + product
    return total


def split(array):
    return jnp.split(array, CHUNKS, axis=1)


def dot(value, weight):
    return jnp.dot(value, weight, preferred_element_type=F32)


def streamed_kernel(dims, depth, x_ref, w_ref, o_ref):
    o_ref[...] = lax.dot_general(
        x_ref[:, :depth], w_ref[...], dims, preferred_element_type=F32
    ).astype(o_ref.dtype)


def streamed(value, weight, transposed, dtype):
    rows = value.shape[0]
    width, depth = weight.shape if transposed else weight.shape[::-1]
    block = next(b for b in (512, 384, 256, 128) if width % b == 0 and b * depth <= BLOCK)
    if transposed:
        dims, w_spec = (((1,), (1,)), ((), ())), pl.BlockSpec((block, depth), lambda i: (i, 0))
    else:
        dims, w_spec = (((1,), (0,)), ((), ())), pl.BlockSpec((depth, block), lambda i: (0, i))
    return pl.pallas_call(
        functools.partial(streamed_kernel, dims, depth),
        grid=(width // block,),
        in_specs=[pl.BlockSpec(value.shape, lambda i: (0, 0)), w_spec],
        out_specs=pl.BlockSpec((rows, block), lambda i: (0, i)),
        out_shape=jax.ShapeDtypeStruct((rows, width), dtype),
        compiler_params=pltpu.CompilerParams(vmem_limit_bytes=24 * 2**20),
        cost_estimate=pl.CostEstimate(
            flops=2 * rows * width * depth,
            bytes_accessed=2 * (width * depth + rows * depth) + 4 * rows * width,
            transcendentals=0,
        ),
    )(value, weight)


def softmax_rows(query, keys, key_mask):
    scores = jnp.einsum("bqd,brd->bqr", query, keys, preferred_element_type=F32) * HD ** (-0.5)
    scores = jnp.where(key_mask[:, None, :], scores, -1e30)
    raised = jnp.exp(scores - jnp.max(scores, axis=-1, keepdims=True))
    return raised / jnp.sum(raised, axis=-1, keepdims=True)


def attend_back(query, mixed_cot, keys, values, key_mask):
    probs = softmax_rows(query, keys, key_mask)
    prob_cot = jnp.einsum("bqd,brd->bqr", mixed_cot, values, preferred_element_type=F32)
    score_cot = (
        probs * (prob_cot - jnp.sum(prob_cot * probs, axis=-1, keepdims=True)) * HD ** (-0.5)
    ).astype(BF)
    query_cot = jnp.einsum("bqr,brd->bqd", score_cot, keys, preferred_element_type=F32).astype(BF)
    key_cot = jnp.einsum("bqr,bqd->brd", score_cot, query, preferred_element_type=F32)
    value_cot = jnp.einsum("bqr,bqd->brd", probs.astype(BF), mixed_cot, preferred_element_type=F32)
    return query_cot, jnp.concatenate([key_cot, value_cot], axis=-1).astype(BF)


def times_transposed(value, weight):
    return lax.dot_general(value, weight, (((1,), (1,)), ((), ())), preferred_element_type=F32)


def local(
    images,
    ln_gain,
    projector,
    tile_counts,
    assign,
    text,
    text_start,
    w_query,
    w_key,
    w_value,
    w_out,
    gates,
    grad_out,
):
    segments = lax.axis_size("segment")
    groups = lax.axis_size("dp")
    members = lax.axis_size("mp")
    segment_id = lax.axis_index("segment")
    group_id = lax.axis_index("dp")
    member_id = lax.axis_index("mp")
    micro, length, feat_width = text.shape
    rows_img, proj_in = images.shape[1:]
    last_width = ln_gain.shape[0]
    query_width = w_query.shape[2]
    share = rows_img // members
    tokens = micro * length
    first = segment_id == 0
    gate_value = jnp.tanh(gates[0])
    query_weight, out_weight = w_query[0], w_out[0]
    key_weight, value_weight = w_key[0], w_value[0]
    kv_width = key_weight.shape[1]

    own_rows = lax.dynamic_slice_in_dim(images[0], member_id * share, share, 0)
    last_cols = own_rows[:, :last_width].astype(F32)
    center = last_cols - jnp.mean(last_cols, axis=-1, keepdims=True)
    inv_std = lax.rsqrt(jnp.mean(center * center, axis=-1, keepdims=True) + 1e-05)
    normed = center * inv_std
    tile_rows = jnp.concatenate([(normed * ln_gain).astype(BF), own_rows[:, last_width:]], axis=1)

    proj_pad = (-proj_in) % LANES or LANES
    facts = jnp.concatenate([assign, tile_counts]).astype(BF)
    facts = jnp.broadcast_to(facts[None], (share, 2))
    sent = jnp.concatenate(
        [tile_rows, jnp.pad(facts, ((0, 0), (0, proj_pad - 2)))], axis=1
    )
    column = lax.all_gather(sent, "dp", axis=0, tiled=False)
    there = column[:, 0, proj_in].astype(jnp.int32)
    source = jnp.argmax(there // micro == group_id).astype(jnp.int32)
    arrived = lax.all_gather(pick(column, source), ("segment", "mp"), axis=0, tiled=True)
    arrived_facts = arrived.reshape(segments, rows_img, -1)[:, 0, proj_in:].astype(jnp.int32)
    slot_of = arrived_facts[:, 0] % micro
    tiles_of = arrived_facts[:, 1]

    seq_ids = jnp.arange(micro, dtype=jnp.int32)
    chosen = slot_of[None, :] == seq_ids[:, None]
    image_seg = jnp.argmax(chosen, axis=1).astype(jnp.int32)
    counts = jnp.sum(jnp.where(chosen, tiles_of[None, :], 0), axis=1)
    key_mask = jnp.arange(rows_img, dtype=jnp.int32)[None, :] < counts[:, None] * PATCH
    text_live = (
        jnp.arange(length, dtype=jnp.int32)[None, :] >= text_start[:, None]
    ).astype(F32)
    scale = (gate_value * text_live).reshape(tokens, 1)

    text_rows = text.reshape(tokens, feat_width)
    grad_rows = grad_out.reshape(tokens, feat_width)
    out_cot = (scale * grad_rows.astype(F32)).astype(BF)
    early = lax.cond(
        first,
        lambda: streamed(text_rows, query_weight, False, F32),
        lambda: streamed(out_cot, out_weight, True, F32),
    )
    early_sum = scatter_columns(early).astype(BF)

    def heads(array):
        return array.reshape(micro, -1, HD)

    def flat(array):
        return array.reshape(tokens, -1)

    features = streamed(arrived, projector, False, BF)
    key_part = jnp.dot(features, key_weight, preferred_element_type=F32)
    value_part = jnp.dot(features, value_weight, preferred_element_type=F32)
    per = kv_width // members
    parts = jnp.stack([key_part, value_part]).reshape(2, -1, members, per).transpose(2, 0, 1, 3)
    kv_image = scatter_sum(parts).astype(BF).reshape(2, segments, rows_img, per)
    kv = jnp.stack([pick(kv_image, image_seg[i], 1) for i in range(micro)], axis=1)
    keys, values = kv[0], kv[1]

    probs = softmax_rows(heads(early_sum), keys, key_mask)
    mixed = jnp.einsum("bqr,brd->bqd", probs.astype(BF), values, preferred_element_type=F32)
    projected = gathered_product(flat(mixed.astype(BF)), out_weight, False)
    hidden = [
        swap((t.astype(F32) + scale * p).astype(BF), "segment", 1)
        for t, p in zip(split(text_rows), projected)
    ]

    query_late = scatter_columns(chunked_product(hidden, query_weight, False)).astype(BF)
    query_cot, kv_cot_late = attend_back(
        heads(query_late), heads(early_sum), keys, values, key_mask
    )
    query_back = gathered_product(flat(query_cot), query_weight, True)
    cot_late = [(g.astype(F32) + q).astype(BF) for g, q in zip(split(grad_rows), query_back)]
    cot_in = [swap(c, "segment", 1) for c in cot_late]

    out_cot = [(scale * c.astype(F32)).astype(BF) for c in cot_in]
    mixed_cot = scatter_columns(chunked_product(out_cot, out_weight, True)).astype(BF)
    query_cot, kv_cot_early = attend_back(
        heads(early_sum), heads(mixed_cot), keys, values, key_mask
    )
    kv_cot = jnp.where(first, kv_cot_early, kv_cot_late)
    kv_cot = jnp.stack([pick(kv_cot, slot_of[i]) for i in range(segments)])
    kv_all = lax.all_gather(kv_cot.reshape(segments * rows_img, 2 * per), "mp", axis=0)
    near, far = gather_pairs(flat(query_cot))
    high = member_id // 2
    gathered = jnp.concatenate(
        [jnp.where(high == 0, near, far), jnp.where(high == 0, far, near)], axis=1
    )
    query_back = streamed(gathered, query_weight, True, F32)
    cot_early = (jnp.concatenate(cot_in, axis=1).astype(F32) + query_back).astype(BF)
    grads = jnp.where(first, cot_early, jnp.concatenate(cot_late, axis=1))

    key_all = kv_all[:, :, :per].transpose(1, 0, 2).reshape(-1, kv_width)
    value_all = kv_all[:, :, per:].transpose(1, 0, 2).reshape(-1, kv_width)
    feature_cot = (
        times_transposed(key_all, key_weight) + times_transposed(value_all, value_weight)
    ).astype(BF)
    norm_part = streamed(feature_cot, projector, True, F32)
    parts = norm_part.reshape(segments, members, share, proj_in).transpose(1, 0, 2, 3)
    summed = scatter_sum(parts)
    returned = pick(summed, segment_id) + swap(
        pick(summed, 1 - segment_id).astype(BF), "segment", 1
    ).astype(F32)
    back_pad = (-proj_in) % BACK_LANES
    column = lax.all_gather(
        jnp.pad(returned.astype(BF), ((0, 0), (0, back_pad))), "dp", axis=0, tiled=False
    )
    norm_cot = pick(column, assign[0] // micro)[:, :proj_in].astype(F32)
    scaled = norm_cot[:, :last_width] * ln_gain
    last_grad = inv_std * (
        scaled
        - jnp.mean(scaled, axis=-1, keepdims=True)
        - normed * jnp.mean(scaled * normed, axis=-1, keepdims=True)
    )
    result = jnp.concatenate([last_grad, norm_cot[:, last_width:]], axis=1).astype(BF)
    result = lax.all_gather(result, "mp", axis=0, tiled=True)
    return (grads.reshape(1, micro, length, feat_width), result[None])


def solution(mesh):
    return jax.shard_map(
        local,
        mesh=mesh,
        in_specs=(
            P(("segment", "dp"), None, None),
            P(),
            P(None, "mp"),
            P(("segment", "dp")),
            P(("segment", "dp")),
            P("dp", None, "mp"),
            P("dp"),
            P("segment", "mp", None),
            P("segment", "mp", None),
            P("segment", "mp", None),
            P("segment", None, "mp"),
            P("segment"),
            P("dp", None, "mp"),
        ),
        out_specs=(P("segment", "dp", None, "mp"), P(("segment", "dp"), None, None)),
        check_vma=False,
    )
```

```python
import functools

import jax
import jax.numpy as jnp
from jax import lax
from jax.experimental import pallas as pl
from jax.experimental.pallas import tpu as pltpu
from jax.sharding import PartitionSpec as P

HD = 128
PATCH = 32
CHUNKS = 2
LANES = 128
BACK_LANES = 512
BLOCK = 2**20
BF = jnp.bfloat16
F32 = jnp.float32


def swap(value, axis, bit):
    count = lax.axis_size(axis)
    return lax.ppermute(value, axis, [(i, i ^ bit) for i in range(count)])


def pick(array, index, axis=0):
    return lax.dynamic_index_in_dim(array, index, axis, keepdims=False)


def scatter_sum(parts, axis="mp"):
    index = lax.axis_index(axis)
    low, high = index % 2, index // 2
    pairs = parts.reshape((2, 2) + parts.shape[1:])
    kept = pick(pairs, low, 1) + swap(pick(pairs, 1 - low, 1).astype(BF), axis, 1).astype(F32)
    return pick(kept, high, 0) + swap(pick(kept, 1 - high, 0).astype(BF), axis, 2).astype(F32)


def scatter_columns(part):
    rows, width = part.shape
    count = lax.axis_size("mp")
    index = lax.axis_index("mp")
    low, high = index % 2, index // 2
    n = width // count

    def block(array, k):
        return lax.dynamic_slice_in_dim(array, k * n, n, 1)

    sent = jnp.concatenate([block(part, 1 - low), block(part, 3 - low)], axis=1).astype(BF)
    got = swap(sent, "mp", 1).astype(F32)
    mine = block(part, 2 * high + low) + block(got, high)
    other = block(part, 2 * (1 - high) + low) + block(got, 1 - high)
    return mine + swap(other.astype(BF), "mp", 2).astype(F32)


def gather_pairs(block):
    index = lax.axis_index("mp")
    low = index % 2
    across = swap(block, "mp", 2)
    near = swap(block, "mp", 1)
    far = swap(across, "mp", 1)

    def side_by_side(own, other):
        return jnp.concatenate(
            [jnp.where(low == 0, own, other), jnp.where(low == 0, other, own)], axis=1
        )

    return side_by_side(block, near), side_by_side(across, far)


def gathered_product(block, weight, transposed):
    near, far = gather_pairs(block)
    high = lax.axis_index("mp") // 2
    depth = near.shape[1]
    axis, width = (1, weight.shape[0]) if transposed else (0, weight.shape[1])
    size = width // CHUNKS
    first = lax.dynamic_slice_in_dim(weight, high * depth, depth, axis)
    multiply = times_transposed if transposed else dot
    started = multiply(near, first)
    result = []
    for c in range(CHUNKS):
        corner, shape = [c * size] * 2, [size] * 2
        corner[axis], shape[axis] = (1 - high) * depth, depth
        part = lax.dynamic_slice(weight, corner, shape)
        result.append(started[:, c * size : (c + 1) * size] + multiply(far, part))
    return result


def chunked_product(chunks, weight, transposed):
    size = weight.shape[1 if transposed else 0] // CHUNKS
    total = None
    for c, chunk in enumerate(chunks):
        part = lax.slice_in_dim(weight, c * size, (c + 1) * size, axis=1 if transposed else 0)
        product = (times_transposed if transposed else dot)(chunk, part)
        total = product if total is None else total + product
    return total


def split(array):
    return jnp.split(array, CHUNKS, axis=1)


def dot(value, weight):
    return jnp.dot(value, weight, preferred_element_type=F32)


def streamed_kernel(dims, depth, x_ref, w_ref, o_ref):
    o_ref[...] = lax.dot_general(
        x_ref[:, :depth], w_ref[...], dims, preferred_element_type=F32
    ).astype(o_ref.dtype)


def streamed(value, weight, transposed, dtype):
    rows = value.shape[0]
    width, depth = weight.shape if transposed else weight.shape[::-1]
    block = next(b for b in (512, 384, 256, 128) if width % b == 0 and b * depth <= BLOCK)
    if transposed:
        dims, w_spec = (((1,), (1,)), ((), ())), pl.BlockSpec((block, depth), lambda i: (i, 0))
    else:
        dims, w_spec = (((1,), (0,)), ((), ())), pl.BlockSpec((depth, block), lambda i: (0, i))
    return pl.pallas_call(
        functools.partial(streamed_kernel, dims, depth),
        grid=(width // block,),
        in_specs=[pl.BlockSpec(value.shape, lambda i: (0, 0)), w_spec],
        out_specs=pl.BlockSpec((rows, block), lambda i: (0, i)),
        out_shape=jax.ShapeDtypeStruct((rows, width), dtype),
        compiler_params=pltpu.CompilerParams(vmem_limit_bytes=52 * 2**20),
        cost_estimate=pl.CostEstimate(
            flops=2 * rows * width * depth,
            bytes_accessed=2 * (width * depth + rows * depth) + 4 * rows * width,
            transcendentals=0,
        ),
    )(value, weight)


def softmax_rows(query, keys, key_mask):
    scores = jnp.einsum("bqd,brd->bqr", query, keys, preferred_element_type=F32) * HD ** (-0.5)
    scores = jnp.where(key_mask[:, None, :], scores, -1e30)
    raised = jnp.exp(scores - jnp.max(scores, axis=-1, keepdims=True))
    return raised / jnp.sum(raised, axis=-1, keepdims=True)


def attend_back(query, mixed_cot, keys, values, key_mask):
    probs = softmax_rows(query, keys, key_mask)
    prob_cot = jnp.einsum("bqd,brd->bqr", mixed_cot, values, preferred_element_type=F32)
    score_cot = (
        probs * (prob_cot - jnp.sum(prob_cot * probs, axis=-1, keepdims=True)) * HD ** (-0.5)
    ).astype(BF)
    query_cot = jnp.einsum("bqr,brd->bqd", score_cot, keys, preferred_element_type=F32).astype(BF)
    key_cot = jnp.einsum("bqr,bqd->brd", score_cot, query, preferred_element_type=F32)
    value_cot = jnp.einsum("bqr,bqd->brd", probs.astype(BF), mixed_cot, preferred_element_type=F32)
    return query_cot, jnp.concatenate([key_cot, value_cot], axis=-1).astype(BF)


def times_transposed(value, weight):
    return lax.dot_general(value, weight, (((1,), (1,)), ((), ())), preferred_element_type=F32)


def local(
    images,
    ln_gain,
    projector,
    tile_counts,
    assign,
    text,
    text_start,
    w_query,
    w_key,
    w_value,
    w_out,
    gates,
    grad_out,
):
    segments = lax.axis_size("segment")
    groups = lax.axis_size("dp")
    members = lax.axis_size("mp")
    segment_id = lax.axis_index("segment")
    group_id = lax.axis_index("dp")
    member_id = lax.axis_index("mp")
    micro, length, feat_width = text.shape
    rows_img, proj_in = images.shape[1:]
    last_width = ln_gain.shape[0]
    query_width = w_query.shape[2]
    share = rows_img // members
    tokens = micro * length
    first = segment_id == 0
    gate_value = jnp.tanh(gates[0])
    query_weight, out_weight = w_query[0], w_out[0]
    key_weight, value_weight = w_key[0], w_value[0]
    kv_width = key_weight.shape[1]

    own_rows = lax.dynamic_slice_in_dim(images[0], member_id * share, share, 0)
    last_cols = own_rows[:, :last_width].astype(F32)
    center = last_cols - jnp.mean(last_cols, axis=-1, keepdims=True)
    inv_std = lax.rsqrt(jnp.mean(center * center, axis=-1, keepdims=True) + 1e-05)
    normed = center * inv_std
    tile_rows = jnp.concatenate([(normed * ln_gain).astype(BF), own_rows[:, last_width:]], axis=1)

    proj_pad = (-proj_in) % LANES or LANES
    facts = jnp.concatenate([assign, tile_counts]).astype(BF)
    facts = jnp.broadcast_to(facts[None], (share, 2))
    sent = jnp.concatenate(
        [tile_rows, jnp.pad(facts, ((0, 0), (0, proj_pad - 2)))], axis=1
    )
    column = lax.all_gather(sent, "dp", axis=0, tiled=False)
    there = column[:, 0, proj_in].astype(jnp.int32)
    source = jnp.argmax(there // micro == group_id).astype(jnp.int32)
    arrived = lax.all_gather(pick(column, source), ("segment", "mp"), axis=0, tiled=True)
    arrived_facts = arrived.reshape(segments, rows_img, -1)[:, 0, proj_in:].astype(jnp.int32)
    slot_of = arrived_facts[:, 0] % micro
    tiles_of = arrived_facts[:, 1]

    seq_ids = jnp.arange(micro, dtype=jnp.int32)
    chosen = slot_of[None, :] == seq_ids[:, None]
    image_seg = jnp.argmax(chosen, axis=1).astype(jnp.int32)
    counts = jnp.sum(jnp.where(chosen, tiles_of[None, :], 0), axis=1)
    key_mask = jnp.arange(rows_img, dtype=jnp.int32)[None, :] < counts[:, None] * PATCH
    text_live = (
        jnp.arange(length, dtype=jnp.int32)[None, :] >= text_start[:, None]
    ).astype(F32)
    scale = (gate_value * text_live).reshape(tokens, 1)

    text_rows = text.reshape(tokens, feat_width)
    grad_rows = grad_out.reshape(tokens, feat_width)
    out_cot = (scale * grad_rows.astype(F32)).astype(BF)
    early = lax.cond(
        first,
        lambda: dot(text_rows, query_weight),
        lambda: times_transposed(out_cot, out_weight),
    )
    early_sum = scatter_columns(early).astype(BF)

    def heads(array):
        return array.reshape(micro, -1, HD)

    def flat(array):
        return array.reshape(tokens, -1)

    features = streamed(arrived, projector, False, BF)
    key_part = jnp.dot(features, key_weight, preferred_element_type=F32)
    value_part = jnp.dot(features, value_weight, preferred_element_type=F32)
    per = kv_width // members
    parts = jnp.stack([key_part, value_part]).reshape(2, -1, members, per).transpose(2, 0, 1, 3)
    kv_image = scatter_sum(parts).astype(BF).reshape(2, segments, rows_img, per)
    kv = jnp.stack([pick(kv_image, image_seg[i], 1) for i in range(micro)], axis=1)
    keys, values = kv[0], kv[1]

    probs = softmax_rows(heads(early_sum), keys, key_mask)
    mixed = jnp.einsum("bqr,brd->bqd", probs.astype(BF), values, preferred_element_type=F32)
    projected = gathered_product(flat(mixed.astype(BF)), out_weight, False)
    hidden = [
        swap((t.astype(F32) + scale * p).astype(BF), "segment", 1)
        for t, p in zip(split(text_rows), projected)
    ]

    query_late = scatter_columns(chunked_product(hidden, query_weight, False)).astype(BF)
    query_cot, kv_cot_late = attend_back(
        heads(query_late), heads(early_sum), keys, values, key_mask
    )
    query_back = gathered_product(flat(query_cot), query_weight, True)
    cot_late = [(g.astype(F32) + q).astype(BF) for g, q in zip(split(grad_rows), query_back)]
    cot_in = [swap(c, "segment", 1) for c in cot_late]

    out_cot = [(scale * c.astype(F32)).astype(BF) for c in cot_in]
    mixed_cot = scatter_columns(chunked_product(out_cot, out_weight, True)).astype(BF)
    query_cot, kv_cot_early = attend_back(
        heads(early_sum), heads(mixed_cot), keys, values, key_mask
    )
    kv_cot = jnp.where(first, kv_cot_early, kv_cot_late)
    kv_cot = jnp.stack([pick(kv_cot, slot_of[i]) for i in range(segments)])
    kv_all = lax.all_gather(kv_cot.reshape(segments * rows_img, 2 * per), "mp", axis=0)
    key_all = kv_all[:, :, :per].transpose(1, 0, 2).reshape(-1, kv_width)
    value_all = kv_all[:, :, per:].transpose(1, 0, 2).reshape(-1, kv_width)
    feature_cot = (
        times_transposed(key_all, key_weight) + times_transposed(value_all, value_weight)
    ).astype(BF)
    norm_part = streamed(feature_cot, projector, True, F32)
    parts = norm_part.reshape(segments, members, share, proj_in).transpose(1, 0, 2, 3)
    summed, query_cot = lax.optimization_barrier((scatter_sum(parts), query_cot))
    returned = pick(summed, segment_id) + swap(
        pick(summed, 1 - segment_id).astype(BF), "segment", 1
    ).astype(F32)
    near, far = gather_pairs(flat(query_cot))
    high = member_id // 2
    gathered = jnp.concatenate(
        [jnp.where(high == 0, near, far), jnp.where(high == 0, far, near)], axis=1
    )
    query_back = streamed(gathered, query_weight, True, F32)
    cot_early = (jnp.concatenate(cot_in, axis=1).astype(F32) + query_back).astype(BF)
    grads = jnp.where(first, cot_early, jnp.concatenate(cot_late, axis=1))

    back_pad = (-proj_in) % BACK_LANES
    column = lax.all_gather(
        jnp.pad(returned.astype(BF), ((0, 0), (0, back_pad))), "dp", axis=0, tiled=False
    )
    norm_cot = pick(column, assign[0] // micro)[:, :proj_in].astype(F32)
    scaled = norm_cot[:, :last_width] * ln_gain
    last_grad = inv_std * (
        scaled
        - jnp.mean(scaled, axis=-1, keepdims=True)
        - normed * jnp.mean(scaled * normed, axis=-1, keepdims=True)
    )
    result = jnp.concatenate([last_grad, norm_cot[:, last_width:]], axis=1).astype(BF)
    result = lax.all_gather(result, "mp", axis=0, tiled=True)
    return (grads.reshape(1, micro, length, feat_width), result[None])


def solution(mesh):
    return jax.shard_map(
        local,
        mesh=mesh,
        in_specs=(
            P(("segment", "dp"), None, None),
            P(),
            P(None, "mp"),
            P(("segment", "dp")),
            P(("segment", "dp")),
            P("dp", None, "mp"),
            P("dp"),
            P("segment", "mp", None),
            P("segment", "mp", None),
            P("segment", "mp", None),
            P("segment", None, "mp"),
            P("segment"),
            P("dp", None, "mp"),
        ),
        out_specs=(P("segment", "dp", None, "mp"), P(("segment", "dp"), None, None)),
        check_vma=False,
    )
```
